32 devices in a mesh: depth: 4 (over y, x), lat: 8 (over z, core).
Axes of the slice: x: 2, y: 2, z: 4, core: 2. Of those that a mesh axis runs over, the one named last changes fastest.
Arguments:
- probe: float32 [2, 256, 256], replicated, may hold values from -4 to 4
- prop_phase: float32 [256, 256], replicated, may hold values from -3.140625 to 3.140625
- object_field: float32 [2, 8, 2048, 1024], P(None, 'depth', 'lat'), may hold values from -1.2 to 2.1, as said below
- measured: float32 [16, 256, 256], P('lat'), may hold values from 0 to 2
- offsets: int32 [16, 2], P('lat'), may hold values from 0 to 1792, as said below
Outputs:
- object_gradient: float32 [2, 8, 2048, 1024], P(None, 'depth', 'lat')
The draws below stay inside these ranges and needn't reach their ends.
Inputs may be any that keep to these rules, and one draw needn't show every extreme that they name: object_field holds each slice's complex transmission, real part first. `offsets`: row j holds the first row and first column of position j's 256 x 256 patch, which lies inside the object; the first row lies in row tile j // 2 or in the tile before it, tile k being rows k * 256 to (k + 1) * 256 - 1.
All inputs are finite; a program needn't handle non-finite values.
Results may differ from the reference program's by a relative error of at most 0.0003.
Values sent between devices are 32-bit elements; how exact they have to be, the bound alone decides.
A program may use at most 128 MiB of HBM per device.

```python
import math
import jax
import jax.numpy as jnp
from jax import lax

PS = 256
POS_DEV = 2
OX = 1024
SLICES = 8
OY = 2048
NPOS = 16


def draw_object_field(key, part):
    shape_all = (2, SLICES, OY, OX)
    centre = jnp.array([0.9, 0.0], jnp.float32).reshape(2, 1, 1, 1)
    spread = jnp.clip(jax.random.normal(key, shape_all, jnp.float32), -4.0, 4.0)
    values = centre + 0.3 * spread
    return values.astype(jnp.float32)


def draw_offsets(key, part):
    tile_count = NPOS // POS_DEV
    row_ids = jnp.arange(NPOS, dtype=jnp.int32)
    owner_ids = row_ids // POS_DEV
    step_back = jax.random.randint(jax.random.fold_in(key, 11), (NPOS,), 0, 2, dtype=jnp.int32)
    step_back = jnp.where(row_ids == NPOS - 1, 0, step_back)
    home_tile = jnp.clip(owner_ids - step_back, 0, tile_count - 1)
    inner_row = jax.random.randint(jax.random.fold_in(key, 12), (NPOS,), 0, PS, dtype=jnp.int32)
    inner_row = jnp.where(row_ids == 0, 0, inner_row)
    inner_row = jnp.where(row_ids == NPOS - 1, PS - 1, inner_row)
    row_offset = jnp.minimum(home_tile * PS + inner_row, OY - PS)
    col_offset = jax.random.randint(jax.random.fold_in(key, 13), (NPOS,), 0, OX - PS + 1, dtype=jnp.int32)
    return jnp.stack([row_offset, col_offset], axis=1).astype(jnp.int32)


def shard_levels(stream_key, shape, cuts, least, largest):
    def one(dim, shards_of):
        draws = jax.random.uniform(jax.random.fold_in(jax.random.fold_in(stream_key, 6), dim), (shards_of,), jnp.float32, least / len(cuts), largest / len(cuts))
        return jnp.repeat(jnp.exp(draws), shape[dim] // shards_of).reshape((-1,) + (1,) * (len(shape) - dim - 1))

    gain = one(*cuts[0])
    for cut in cuts[1:]:
        gain = gain * one(*cut)
    return gain


def centred(key, dims, deviation, most, held_as=jnp.bfloat16):
    return jnp.clip(deviation * jax.random.normal(key, dims, jnp.float32), -most, most).astype(held_as)


def setup_inputs(seed: int = 0) -> dict:
    key_of = jax.random.split(jax.random.key(seed), 6)
    probe = centred(key_of[0], (2, PS, PS), 0.7, 4.0, jnp.float32)
    prop_phase = jnp.clip(jax.random.uniform(key_of[1], (PS, PS), jnp.float32, -3.140625, 3.140625), -3.140625, 3.140625)
    object_field = draw_object_field(jax.random.fold_in(key_of[5], 71), 0)
    measured = jnp.clip(2.0 * jax.random.uniform(key_of[3], (NPOS, PS, PS), jnp.float32) ** shard_levels(key_of[3], (NPOS, PS, PS), ((0, 8),), -0.2, 0.2), 0.0, 2.0)
    offsets = draw_offsets(jax.random.fold_in(key_of[5], 71), 0)
    return {"probe": probe, "prop_phase": prop_phase, "object_field": object_field, "measured": measured, "offsets": offsets}


def dft_tables(length):
    counter = jnp.arange(length, dtype=jnp.int32)
    phase = counter[:, None] * counter[None, :] % length
    angle = phase.astype(jnp.float32) * (2.0 * math.pi / length)
    factor = 1.0 / math.sqrt(length)
    return (jnp.cos(angle) * factor, jnp.sin(angle) * factor)

def matmul_exact(left, right):
    return jnp.matmul(left, right, precision=lax.Precision.HIGHEST)

def transform(values, cosine, sine, direction):
    re_part = values[..., 0, :, :]
    im_part = values[..., 1, :, :]
    left_re = matmul_exact(cosine, re_part) - direction * matmul_exact(sine, im_part)
    left_im = matmul_exact(cosine, im_part) + direction * matmul_exact(sine, re_part)
    out_re = matmul_exact(left_re, cosine) - direction * matmul_exact(left_im, sine)
    out_im = matmul_exact(left_im, cosine) + direction * matmul_exact(left_re, sine)
    return jnp.stack([out_re, out_im], axis=-3)

def complex_product(first, second):
    first_re = first[..., 0, :, :]
    first_im = first[..., 1, :, :]
    second_re = second[..., 0, :, :]
    second_im = second[..., 1, :, :]
    return jnp.stack([first_re * second_re - first_im * second_im, first_re * second_im + first_im * second_re], axis=-3)

def conj_product(first, second):
    first_re = first[..., 0, :, :]
    first_im = first[..., 1, :, :]
    second_re = second[..., 0, :, :]
    second_im = second[..., 1, :, :]
    return jnp.stack([first_re * second_re + first_im * second_im, first_re * second_im - first_im * second_re], axis=-3)

def propagate(values, kernel, cosine, sine, adjoint):
    spectrum = transform(values, cosine, sine, -1.0)
    if adjoint:
        spectrum = conj_product(kernel, spectrum)
    else:
        spectrum = complex_product(kernel, spectrum)
    return transform(spectrum, cosine, sine, 1.0)

def reference(probe, prop_phase, object_field, measured, offsets):
    cosine, sine = dft_tables(PS)
    kernel = jnp.stack([jnp.cos(prop_phase), jnp.sin(prop_phase)], axis=0)
    zero_index = jnp.zeros((), jnp.int32)

    def forward_step(wavefield, transmit):
        exiting = complex_product(transmit, wavefield)
        return (propagate(exiting, kernel, cosine, sine, False), wavefield)

    def backward_step(adjoint, transmit):
        moved = conj_product(transmit, adjoint)
        earlier = propagate(moved, kernel, cosine, sine, True)
        return (earlier, earlier)

    def position_terms(position):
        row_offset = offsets[position, 0].astype(jnp.int32)
        col_offset = offsets[position, 1].astype(jnp.int32)
        window = lax.dynamic_slice(object_field, (zero_index, zero_index, row_offset, col_offset), (2, SLICES, PS, PS))
        window = jnp.transpose(window, (1, 0, 2, 3))
        wavefield, entering = lax.scan(forward_step, probe, window[:-1])
        entering = jnp.concatenate([entering, wavefield[None]], axis=0)
        exiting = complex_product(window[-1], wavefield)
        farfield = transform(exiting, cosine, sine, -1.0)
        intensity = farfield[0] * farfield[0] + farfield[1] * farfield[1]
        misfit = intensity - measured[position]
        adjoint = transform(misfit[None] * farfield, cosine, sine, 1.0)
        unused, earlier = lax.scan(backward_step, adjoint, window[1:], reverse=True)
        adjoints = jnp.concatenate([earlier, adjoint[None]], axis=0)
        terms = conj_product(entering, adjoints)
        return (jnp.transpose(terms, (1, 0, 2, 3)), row_offset, col_offset)

    def accumulate(total, position):
        terms, row_offset, col_offset = position_terms(position)
        start = (zero_index, zero_index, row_offset, col_offset)
        current = lax.dynamic_slice(total, start, (2, SLICES, PS, PS))
        return (lax.dynamic_update_slice(total, current + terms, start), None)
    initial = jnp.zeros((2, SLICES, OY, OX), jnp.float32)
    total, unused = lax.scan(accumulate, initial, jnp.arange(NPOS, dtype=jnp.int32))
    return total
```

```python
import functools
import math

import jax
import jax.numpy as jnp
import ml_dtypes
import numpy as np
from jax import lax
from jax.experimental import pallas as pl
from jax.experimental.pallas import tpu as pltpu
from jax.sharding import PartitionSpec as P


def dft_tables(length):
    counter = np.arange(length)
    angle = (counter[:, None] * counter[None, :] % length) * (2.0 * math.pi / length)
    cosine, sine = np.cos(angle) / math.sqrt(length), np.sin(angle) / math.sqrt(length)
    values = np.stack([cosine, cosine + sine, cosine - sine])
    high = values.astype(ml_dtypes.bfloat16)
    low = (values - high.astype(np.float64)).astype(ml_dtypes.bfloat16)
    return jnp.asarray(np.stack([high, low]))


def split(x):
    high = x.astype(jnp.bfloat16)
    low = (x - high.astype(jnp.float32)).astype(jnp.bfloat16)
    return high, low


def dot(a, b):
    return jnp.dot(a, b, preferred_element_type=jnp.float32)


def three_dot(a, b):
    return dot(a[0], b[0]) + (dot(a[0], b[1]) + dot(a[1], b[0]))


def side(re, im, tables, inverse, left):
    def table(i):
        return tables[0, i], tables[1, i]

    def product(x, i):
        x = split(x)
        return three_dot(table(i), x) if left else three_dot(x, table(i))

    first, second = (2, 1) if inverse else (1, 2)
    both = product(re + im, 0)
    return both - product(im, second), both - product(re, first)


def transform(re, im, tables, inverse):
    re, im = side(re, im, tables, inverse, False)
    return side(re, im, tables, inverse, True)


def inverse_transform(re, im, tables):
    re, im = side(re, im, tables, True, True)
    return side(re, im, tables, True, False)


def wave_kernel(active_ref, probe, wave_table, tables, measured, patches, terms, psi, held):
    count = patches.shape[0]

    @pl.when(active_ref[0] == 1)
    def _():
        held[0] = probe[0]
        held[1] = probe[1]

        def exit_wave(s):
            a, b = held[0], held[1]
            psi[s, 0] = a
            psi[s, 1] = b
            c, d = patches[s, 0], patches[s, 1]
            return c * a - d * b, c * b + d * a

        def propagate(re, im, sign):
            re, im = transform(re, im, tables, False)
            hr, hi = wave_table[0], wave_table[1]
            if sign > 0:
                re, im = hr * re - hi * im, hr * im + hi * re
            else:
                re, im = hr * re + hi * im, hr * im - hi * re
            re, im = inverse_transform(re, im, tables)
            held[0] = re
            held[1] = im

        @pl.loop(0, count - 1)
        def _(s):
            re, im = exit_wave(s)
            propagate(re, im, 1)

        re, im = exit_wave(count - 1)
        re, im = transform(re, im, tables, False)
        misfit = re * re + im * im - measured[...]
        re, im = inverse_transform(misfit * re, misfit * im, tables)
        held[0] = re
        held[1] = im

        def term(s):
            a, b = held[0], held[1]
            c, d = psi[s, 0], psi[s, 1]
            terms[s, 0] = c * a + d * b
            terms[s, 1] = c * b - d * a
            return a, b

        @pl.loop(0, count - 1)
        def _(i):
            s = count - 1 - i
            a, b = term(s)
            c, d = patches[s, 0], patches[s, 1]
            propagate(c * a + d * b, c * b - d * a, -1)

        term(0)


def local(probe, prop_phase, object_field, measured, offsets):
    width = probe.shape[-1]
    slab = object_field.shape[1]
    columns = object_field.shape[3]
    blocks = columns // width
    owned = offsets.shape[0]
    depth_count = lax.axis_size("depth")
    lat_count = lax.axis_size("lat")
    depth = lax.axis_index("depth")
    lat = lax.axis_index("lat")
    tables = dft_tables(width)
    wave_table = jnp.stack([jnp.cos(prop_phase), jnp.sin(prop_phase)])
    rows = lax.broadcasted_iota(jnp.int32, (width, width), 0)
    lanes = lax.broadcasted_iota(jnp.int32, (width, width), 1)

    up = [(i, i + 1) for i in range(lat_count - 1)]
    down = [(i + 1, i) for i in range(lat_count - 1)]
    offsets_below = lax.ppermute(offsets, "lat", up)
    offsets_above = lax.ppermute(offsets, "lat", down)

    def row_mask(row):
        start = row - lat * width
        return (rows >= start) & (rows < start + width)

    def piece(offset):
        mask = row_mask(offset[0])
        block = offset[1] // width
        rest = offset[1] % width
        zero = jnp.zeros((), jnp.int32)
        shape = object_field.shape[:3] + (width,)
        first = lax.dynamic_slice(object_field, (zero, zero, zero, block * width), shape)
        block = jnp.minimum(block + 1, blocks - 1)
        second = lax.dynamic_slice(object_field, (zero, zero, zero, block * width), shape)
        return jnp.where(mask, jnp.where(lanes >= rest, first, second), 0.0)

    def pieces(of):
        return jnp.stack([piece(of[i]) for i in range(owned)])

    from_below = lax.ppermute(pieces(offsets_above), "lat", up)
    from_above = lax.ppermute(pieces(offsets_below), "lat", down)
    mine = pieces(offsets) + from_below + from_above

    names = ("depth", "lat")

    def pairs(step, back):
        out = []
        for k in range(lat_count):
            for p in range(owned):
                e = (k * owned + p) % depth_count
                d = (e + step) % depth_count
                pair = (d * lat_count + k, e * lat_count + k)
                out.append(pair[::-1] if back else pair)
        return out

    def slot(e):
        return (e - lat * owned) % depth_count

    mine_slot = slot(depth)
    active = mine_slot < owned
    position = jnp.minimum(mine_slot, owned - 1)

    def of_position(array, p):
        return lax.dynamic_index_in_dim(array, jnp.minimum(p, owned - 1), 0, keepdims=False)

    parts = jnp.zeros((depth_count, 2, slab, width, width), jnp.float32)
    parts = lax.dynamic_update_index_in_dim(parts, of_position(mine, mine_slot), depth, 0)
    for step in range(1, depth_count):
        target = (depth - step) % depth_count
        got = lax.ppermute(of_position(mine, slot(target)), names, pairs(step, False))
        parts = lax.dynamic_update_index_in_dim(parts, got, (depth + step) % depth_count, 0)
    patches = jnp.transpose(parts, (0, 2, 1, 3, 4)).reshape(-1, 2, width, width)

    offset = of_position(offsets, mine_slot)
    rolled = jnp.roll(probe, (offset[0] % width, offset[1] % width), (1, 2))
    terms = pl.pallas_call(
        wave_kernel,
        out_shape=jax.ShapeDtypeStruct(patches.shape, jnp.float32),
        in_specs=[pl.BlockSpec(memory_space=pltpu.SMEM)]
        + [pl.BlockSpec(memory_space=pltpu.VMEM)] * 5,
        out_specs=pl.BlockSpec(memory_space=pltpu.VMEM),
        scratch_shapes=[
            pltpu.VMEM(patches.shape, jnp.float32),
            pltpu.VMEM(patches.shape[1:], jnp.float32),
        ],
        compiler_params=pltpu.CompilerParams(vmem_limit_bytes=48 * 1024 * 1024),
    )(
        active.astype(jnp.int32)[None],
        rolled,
        wave_table,
        tables,
        of_position(measured, mine_slot),
        patches,
    )
    terms = jnp.transpose(terms.reshape(depth_count, slab, 2, width, width), (0, 2, 1, 3, 4))

    zero_terms = jnp.zeros((owned, 2, slab, width, width), jnp.float32)
    own = lax.dynamic_index_in_dim(terms, depth, 0, keepdims=False)
    total_terms = [jnp.where(mine_slot == p, own, 0.0) for p in range(owned)]
    for step in range(1, depth_count):
        target = (depth + step) % depth_count
        got = lax.ppermute(
            lax.dynamic_index_in_dim(terms, target, 0, keepdims=False), names, pairs(step, True)
        )
        source = slot((depth - step) % depth_count)
        total_terms = [jnp.where(source == p, got, t) for p, t in enumerate(total_terms)]
    mine_terms = jnp.stack(total_terms)
    terms_below = lax.ppermute(mine_terms, "lat", up)
    terms_above = lax.ppermute(mine_terms, "lat", down)

    total = [jnp.zeros(object_field.shape[:3] + (width,), jnp.float32) for _ in range(blocks)]
    sources = ((offsets, mine_terms), (offsets_below, terms_below), (offsets_above, terms_above))
    for rank, (of, values) in enumerate(sources):
        exists = (lat > 0) if rank == 1 else (lat < lat_count - 1) if rank == 2 else True
        for p in range(owned):
            mask = row_mask(of[p, 0]) & exists
            block = of[p, 1] // width
            rest = of[p, 1] % width
            for b in range(blocks):
                here = ((block == b) & (lanes >= rest)) | ((block + 1 == b) & (lanes < rest))
                total[b] = total[b] + jnp.where(mask & here, values[p], 0.0)
    return jnp.concatenate(total, axis=3)


def solution(mesh):
    in_specs = (P(), P(), P(None, "depth", "lat", None), P("lat", None, None), P("lat", None))
    out_specs = P(None, "depth", "lat", None)
    return jax.shard_map(local, mesh=mesh, in_specs=in_specs, out_specs=out_specs, check_vma=False)
```

```python
import functools
import math

import jax
import jax.numpy as jnp
import ml_dtypes
import numpy as np
from jax import lax
from jax.experimental import pallas as pl
from jax.experimental.pallas import tpu as pltpu
from jax.sharding import PartitionSpec as P


def dft_tables(length):
    counter = np.arange(length)
    angle = (counter[:, None] * counter[None, :] % length) * (2.0 * math.pi / length)
    cosine, sine = np.cos(angle) / math.sqrt(length), np.sin(angle) / math.sqrt(length)
    values = np.stack([cosine, cosine + sine, cosine - sine])
    high = values.astype(ml_dtypes.bfloat16)
    low = (values - high.astype(np.float64)).astype(ml_dtypes.bfloat16)
    return jnp.asarray(np.stack([high, low]))


def split(x):
    high = x.astype(jnp.bfloat16)
    low = (x - high.astype(jnp.float32)).astype(jnp.bfloat16)
    return high, low


def dot(a, b):
    return jnp.dot(a, b, preferred_element_type=jnp.float32)


def three_dot(a, b):
    return dot(a[0], b[0]) + (dot(a[0], b[1]) + dot(a[1], b[0]))


def side(re, im, tables, inverse, left):
    def table(i):
        return tables[0, i], tables[1, i]

    def product(x, i):
        x = split(x)
        return three_dot(table(i), x) if left else three_dot(x, table(i))

    first, second = (2, 1) if inverse else (1, 2)
    both = product(re + im, 0)
    return both - product(im, second), both - product(re, first)


def transform(re, im, tables, inverse):
    re, im = side(re, im, tables, inverse, False)
    return side(re, im, tables, inverse, True)


def inverse_transform(re, im, tables):
    re, im = side(re, im, tables, True, True)
    return side(re, im, tables, True, False)


def row_mask(row, lat, width):
    rows = lax.broadcasted_iota(jnp.int32, (width, width), 0)
    start = row - lat * width
    return (rows >= start) & (rows < start + width)


def extract_kernel(place, offsets, field, mine, to_up, to_down):
    width = field.shape[2]
    blocks = field.shape[3] // width
    lanes = lax.broadcasted_iota(jnp.int32, (width, width), 1)
    for rank, out in enumerate((mine, to_up, to_down)):
        for p in range(mine.shape[0]):
            column = offsets[rank, p, 1]
            block = column // width
            mask = row_mask(offsets[rank, p, 0], place[0], width)
            first = mask & (lanes >= column - block * width)
            second = mask & (lanes < column - block * width)
            after = jnp.minimum(block + 1, blocks - 1)
            for c in range(2):
                a = field[c, 0, :, pl.ds(pl.multiple_of(block * width, width), width)]
                b = field[c, 0, :, pl.ds(pl.multiple_of(after * width, width), width)]
                out[p, 0, c] = jnp.where(first, a, jnp.where(second, b, 0.0))


def deposit_kernel(place, offsets, home, below, above, out):
    width = out.shape[2]
    blocks = out.shape[3] // width
    lanes = lax.broadcasted_iota(jnp.int32, (width, width), 1)
    for b in range(blocks):
        for c in range(2):
            total = jnp.zeros((width, width), jnp.float32)
            for rank, terms in enumerate((home, below, above)):
                for p in range(home.shape[0]):
                    column = offsets[rank, p, 1]
                    block = column // width
                    rest = column - block * width
                    low = jnp.where(block == b, rest, width)
                    high = jnp.where(block + 1 == b, rest, 0)
                    here = (lanes >= low) | (lanes < high)
                    mask = row_mask(offsets[rank, p, 0], place[0], width) & here
                    total += jnp.where(mask, terms[p, 0, c], 0.0)
            out[c, 0, :, b * width : (b + 1) * width] = total


def wave_kernel(
    depth_count, lat_count, probe, wave_table, tables, measured, mine, to_up, to_down,
    home, terms_below, terms_above,
    from_below, from_above, merged, patches, terms, psi, held,
    z_send, z_recv, in_send, in_recv, out_send, out_recv, back_send, back_recv,
):
    depth = lax.axis_index("depth")
    lat = lax.axis_index("lat")
    owned, slab = mine.shape[:2]
    count = depth_count * slab
    has_above = lat < lat_count - 1
    has_below = lat > 0
    slot = lax.rem(depth - lax.rem(lat * owned, depth_count) + depth_count, depth_count)
    active = slot < owned

    def owner(p):
        return lax.rem(lat * owned + p, depth_count)

    barrier = pltpu.get_barrier_semaphore()
    for step in range(1, depth_count):
        other = lax.rem(depth + step, depth_count)
        pl.semaphore_signal(
            barrier, inc=1, device_id=(other, lat), device_id_type=pl.DeviceIdType.MESH
        )

    def greet(other):
        pl.semaphore_signal(
            barrier, inc=1, device_id=(depth, other), device_id_type=pl.DeviceIdType.MESH
        )

    pl.when(has_above)(lambda: greet(lat + 1))
    pl.when(has_below)(lambda: greet(lat - 1))
    peers = depth_count - 1 + has_above.astype(jnp.int32) + has_below.astype(jnp.int32)
    pl.semaphore_wait(barrier, peers)

    def remote(source, target, send, recv, device):
        return pltpu.make_async_remote_copy(
            src_ref=source, dst_ref=target, send_sem=send, recv_sem=recv,
            device_id=device, device_id_type=pl.DeviceIdType.MESH,
        )

    def upward(p, s):
        return remote(to_up.at[p, s], from_below.at[p, s],
                      z_send.at[0, p, s], z_recv.at[0, p, s], (depth, lat + 1))

    def downward(p, s):
        return remote(to_down.at[p, s], from_above.at[p, s],
                      z_send.at[1, p, s], z_recv.at[1, p, s], (depth, lat - 1))

    def inward(p, s):
        place = depth * slab + s
        return remote(merged.at[p, s], patches.at[place],
                      in_send.at[p, s], in_recv.at[place], (owner(p), lat))

    def outward(s):
        layer = lax.rem(s, slab)
        place = jnp.minimum(slot, owned - 1)
        return remote(terms.at[s], home.at[place, layer],
                      out_send.at[s], out_recv.at[place, layer], (s // slab, lat))

    def back_up(p, s):
        return remote(home.at[p, s], terms_below.at[p, s],
                      back_send.at[0, p, s], back_recv.at[0, p, s], (depth, lat + 1))

    def back_down(p, s):
        return remote(home.at[p, s], terms_above.at[p, s],
                      back_send.at[1, p, s], back_recv.at[1, p, s], (depth, lat - 1))

    chunks = [(p, s) for s in range(slab) for p in range(owned)]
    for p, s in chunks:
        pl.when(has_above)(lambda: upward(p, s).start())
        pl.when(has_below)(lambda: downward(p, s).start())
    for p, s in chunks:
        merged[p, s] = mine[p, s]

        @pl.when(has_below)
        def _():
            upward(p, s).wait_recv()
            merged[p, s] += from_below[p, s]

        @pl.when(has_above)
        def _():
            downward(p, s).wait_recv()
            merged[p, s] += from_above[p, s]

        @pl.when(owner(p) == depth)
        def _():
            patches[depth * slab + s] = merged[p, s]

        @pl.when(owner(p) != depth)
        def _():
            inward(p, s).start()

    @pl.when(active)
    def _():
        held[0] = probe[0]
        held[1] = probe[1]

        def exit_wave(s):
            a, b = held[0], held[1]
            psi[s, 0] = a
            psi[s, 1] = b

            @pl.when(s // slab != depth)
            def _():
                remote(merged.at[0, 0], patches.at[s], in_send.at[0, 0],
                       in_recv.at[s], (depth, lat)).wait_recv()

            c, d = patches[s, 0], patches[s, 1]
            return c * a - d * b, c * b + d * a

        def propagate(re, im, sign):
            re, im = transform(re, im, tables, False)
            hr, hi = wave_table[0], wave_table[1]
            if sign > 0:
                re, im = hr * re - hi * im, hr * im + hi * re
            else:
                re, im = hr * re + hi * im, hr * im - hi * re
            re, im = inverse_transform(re, im, tables)
            held[0] = re
            held[1] = im

        @pl.loop(0, count - 1)
        def _(s):
            re, im = exit_wave(s)
            propagate(re, im, 1)

        re, im = exit_wave(count - 1)
        re, im = transform(re, im, tables, False)
        target = measured[0]
        for p in range(1, owned):
            target = jnp.where(slot == p, measured[p], target)
        misfit = re * re + im * im - target
        re, im = inverse_transform(misfit * re, misfit * im, tables)
        held[0] = re
        held[1] = im

        def term(s):
            a, b = held[0], held[1]
            c, d = psi[s, 0], psi[s, 1]
            terms[s, 0] = c * a + d * b
            terms[s, 1] = c * b - d * a

            @pl.when(s // slab != depth)
            def _():
                outward(s).start()

            return a, b

        @pl.loop(0, count - 1)
        def _(i):
            s = count - 1 - i
            a, b = term(s)
            c, d = patches[s, 0], patches[s, 1]
            propagate(c * a + d * b, c * b - d * a, -1)

        term(0)

    back = [(p, s) for s in reversed(range(slab)) for p in range(owned)]
    for p, s in back:

        @pl.when(owner(p) == depth)
        def _():
            home[p, s] = terms[depth * slab + s]

        @pl.when(owner(p) != depth)
        def _():
            remote(terms.at[0], home.at[p, s], out_send.at[0],
                   out_recv.at[p, s], (depth, lat)).wait_recv()

        pl.when(has_above)(lambda: back_up(p, s).start())
        pl.when(has_below)(lambda: back_down(p, s).start())

    for p, s in back:

        @pl.when(has_below)
        def _():
            back_up(p, s).wait_recv()
            downward(p, s).wait_send()
            back_down(p, s).wait_send()

        @pl.when(has_above)
        def _():
            back_down(p, s).wait_recv()
            upward(p, s).wait_send()
            back_up(p, s).wait_send()

        @pl.when(owner(p) != depth)
        def _():
            inward(p, s).wait_send()

    @pl.when(active)
    def _():
        @pl.loop(0, count)
        def _(s):
            @pl.when(s // slab != depth)
            def _():
                outward(s).wait_send()


def local(probe, prop_phase, object_field, measured, offsets):
    width = probe.shape[-1]
    slab, columns = object_field.shape[1], object_field.shape[3]
    owned = offsets.shape[0]
    depth_count = lax.axis_size("depth")
    lat_count = lax.axis_size("lat")
    depth = lax.axis_index("depth")
    lat = lax.axis_index("lat")
    tables = dft_tables(width)
    wave_table = jnp.stack([jnp.cos(prop_phase), jnp.sin(prop_phase)])

    up = [(i, i + 1) for i in range(lat_count - 1)]
    down = [(i + 1, i) for i in range(lat_count - 1)]
    far = -(lat_count + 2) * width
    none = jnp.array([far, 0], jnp.int32) * jnp.ones((owned, 1), jnp.int32)
    below = jnp.where(lat > 0, lax.ppermute(offsets, "lat", up), none)
    above = jnp.where(lat < lat_count - 1, lax.ppermute(offsets, "lat", down), none)
    place = lat.astype(jnp.int32)[None]
    smem = pl.BlockSpec(memory_space=pltpu.SMEM)
    vmem = pl.BlockSpec(memory_space=pltpu.VMEM)
    field_spec = pl.BlockSpec((2, 1, width, columns), lambda s: (0, s, 0, 0))
    piece_spec = pl.BlockSpec((owned, 1, 2, width, width), lambda s: (0, s, 0, 0, 0))
    pieces = jax.ShapeDtypeStruct((owned, slab, 2, width, width), jnp.float32)
    limit = 56 * 1024 * 1024
    mine, to_up, to_down = pl.pallas_call(
        extract_kernel,
        grid=(slab,),
        out_shape=[pieces] * 3,
        in_specs=[smem, smem, field_spec],
        out_specs=[piece_spec] * 3,
        compiler_params=pltpu.CompilerParams(vmem_limit_bytes=limit),
    )(place, jnp.stack([offsets, above, below]), object_field)

    slot = (depth - lat * owned) % depth_count
    offset = lax.dynamic_index_in_dim(offsets, jnp.minimum(slot, owned - 1), 0, keepdims=False)
    rolled = jnp.roll(probe, (offset[0] % width, offset[1] % width), (1, 2))
    layers = (depth_count * slab, 2, width, width)
    dma = pltpu.SemaphoreType.DMA
    home, terms_below, terms_above = pl.pallas_call(
        functools.partial(wave_kernel, depth_count, lat_count),
        out_shape=[pieces] * 3,
        in_specs=[vmem] * 7,
        out_specs=[vmem] * 3,
        scratch_shapes=[pltpu.VMEM(pieces.shape, jnp.float32)] * 3
        + [pltpu.VMEM(layers, jnp.float32)] * 3
        + [
            pltpu.VMEM(layers[1:], jnp.float32),
            dma((2, owned, slab)), dma((2, owned, slab)),
            dma((owned, slab)), dma((layers[0],)),
            dma((layers[0],)), dma((owned, slab)),
            dma((2, owned, slab)), dma((2, owned, slab)),
        ],
        compiler_params=pltpu.CompilerParams(
            vmem_limit_bytes=limit, collective_id=0, has_side_effects=True
        ),
    )(rolled, wave_table, tables, measured, mine, to_up, to_down)

    return pl.pallas_call(
        deposit_kernel,
        grid=(slab,),
        out_shape=jax.ShapeDtypeStruct(object_field.shape, jnp.float32),
        in_specs=[smem, smem] + [piece_spec] * 3,
        out_specs=field_spec,
        compiler_params=pltpu.CompilerParams(vmem_limit_bytes=limit),
    )(place, jnp.stack([offsets, below, above]), home, terms_below, terms_above)


def solution(mesh):
    in_specs = (P(), P(), P(None, "depth", "lat", None), P("lat", None, None), P("lat", None))
    out_specs = P(None, "depth", "lat", None)
    return jax.shard_map(local, mesh=mesh, in_specs=in_specs, out_specs=out_specs, check_vma=False)
```

```python
import functools
import math

import jax
import jax.numpy as jnp
import ml_dtypes
import numpy as np
from jax import lax
from jax.experimental import pallas as pl
from jax.experimental.pallas import tpu as pltpu
from jax.sharding import PartitionSpec as P


def dft_tables(length):
    counter = np.arange(length)
    angle = (counter[:, None] * counter[None, :] % length) * (2.0 * math.pi / length)
    cosine, sine = np.cos(angle) / math.sqrt(length), np.sin(angle) / math.sqrt(length)
    values = np.stack([cosine, cosine + sine, cosine - sine])
    high = values.astype(ml_dtypes.bfloat16)
    low = (values - high.astype(np.float64)).astype(ml_dtypes.bfloat16)
    return jnp.asarray(np.stack([high, low]))


def split(x):
    high = x.astype(jnp.bfloat16)
    low = (x - high.astype(jnp.float32)).astype(jnp.bfloat16)
    return high, low


def dot(a, b):
    return jnp.dot(a, b, preferred_element_type=jnp.float32)


def three_dot(a, b):
    return dot(a[0], b[0]) + (dot(a[0], b[1]) + dot(a[1], b[0]))


def side(re, im, tables, inverse, left):
    def table(i):
        return tables[0, i], tables[1, i]

    def product(x, i):
        x = split(x)
        return three_dot(table(i), x) if left else three_dot(x, table(i))

    first, second = (2, 1) if inverse else (1, 2)
    both = product(re + im, 0)
    return both - product(im, second), both - product(re, first)


def transform(re, im, tables, inverse):
    re, im = side(re, im, tables, inverse, False)
    return side(re, im, tables, inverse, True)


def inverse_transform(re, im, tables):
    re, im = side(re, im, tables, True, True)
    return side(re, im, tables, True, False)


def row_mask(row, lat, width):
    rows = lax.broadcasted_iota(jnp.int32, (width, width), 0)
    start = row - lat * width
    return (rows >= start) & (rows < start + width)


def patch_corner(place, offsets, rank, p):
    row, column = offsets[rank][p, 0], offsets[rank][p, 1]
    if rank == 1:
        row = jnp.where(place[0] > 0, row, place[2])
    if rank == 2:
        row = jnp.where(place[0] < place[1] - 1, row, place[2])
    return row, column


def extract_kernel(
    place, own, below, above, probe, phase, field, mine, to_up, to_down, rolled, wave_table
):
    width = field.shape[2]
    blocks = field.shape[3] // width
    owned = mine.shape[0]
    offsets = (own, below, above)

    @pl.when(pl.program_id(0) == 0)
    def _():
        row, column = own[0, 0], own[0, 1]
        for p in range(1, owned):
            row = jnp.where(place[3] == p, own[p, 0], row)
            column = jnp.where(place[3] == p, own[p, 1], column)
        for c in range(2):
            turned = pltpu.roll(probe[c], lax.rem(row, width), 0)
            rolled[c] = pltpu.roll(turned, lax.rem(column, width), 1)
        wave_table[0] = jnp.cos(phase[...])
        wave_table[1] = jnp.sin(phase[...])

    lanes = lax.broadcasted_iota(jnp.int32, (width, width), 1)
    for rank, out in ((0, mine), (2, to_up), (1, to_down)):
        for p in range(owned):
            row, column = patch_corner(place, offsets, rank, p)
            block = column // width
            mask = row_mask(row, place[0], width)
            first = mask & (lanes >= column - block * width)
            second = mask & (lanes < column - block * width)
            after = jnp.minimum(block + 1, blocks - 1)
            for c in range(2):
                a = field[c, 0, :, pl.ds(pl.multiple_of(block * width, width), width)]
                b = field[c, 0, :, pl.ds(pl.multiple_of(after * width, width), width)]
                out[p, 0, c] = jnp.where(first, a, jnp.where(second, b, 0.0))


def deposit_kernel(place, own, low_tile, high_tile, home, below, above, out):
    width = out.shape[2]
    blocks = out.shape[3] // width
    owned = home.shape[0]
    strip = 32
    lanes = lax.broadcasted_iota(jnp.int32, (strip, width), 1)
    rows = lax.broadcasted_iota(jnp.int32, (strip, width), 0)
    corners = []
    for rank, terms in enumerate((home, below, above)):
        for p in range(owned):
            row, column = patch_corner(place, (own, low_tile, high_tile), rank, p)
            corners.append((terms, p, row - place[0] * width, column // width, column))

    @pl.loop(0, width // strip)
    def _(i):
        here_rows = pl.ds(pl.multiple_of(i * strip, strip), strip)
        at = rows + i * strip
        for b in range(blocks):
            total = [jnp.zeros((strip, width), jnp.float32) for _ in range(2)]
            for terms, p, start, block, column in corners:
                rest = column - block * width
                low = jnp.where(block == b, rest, width)
                high = jnp.where(block + 1 == b, rest, 0)
                mask = (at >= start) & (at < start + width) & ((lanes >= low) | (lanes < high))
                for c in range(2):
                    total[c] += jnp.where(mask, terms[p, 0, c, here_rows, :], 0.0)
            for c in range(2):
                out[c, 0, here_rows, b * width : (b + 1) * width] = total[c]


def wave_kernel(
    depth_count, lat_count, probe, wave_table, tables, measured, mine, to_up, to_down,
    home, terms_below, terms_above,
    from_below, from_above, merged, patches, terms, psi, held,
    z_send, z_recv, in_send, in_recv, out_send, out_recv, back_send, back_recv,
):
    depth = lax.axis_index("depth")
    lat = lax.axis_index("lat")
    owned, slab = mine.shape[:2]
    count = depth_count * slab
    has_above = lat < lat_count - 1
    has_below = lat > 0
    slot = lax.rem(depth - lax.rem(lat * owned, depth_count) + depth_count, depth_count)
    active = slot < owned

    def owner(p):
        return lax.rem(lat * owned + p, depth_count)

    barrier = pltpu.get_barrier_semaphore()
    for step in range(1, depth_count):
        other = lax.rem(depth + step, depth_count)
        pl.semaphore_signal(
            barrier, inc=1, device_id=(other, lat), device_id_type=pl.DeviceIdType.MESH
        )

    def greet(other):
        pl.semaphore_signal(
            barrier, inc=1, device_id=(depth, other), device_id_type=pl.DeviceIdType.MESH
        )

    pl.when(has_above)(lambda: greet(lat + 1))
    pl.when(has_below)(lambda: greet(lat - 1))
    peers = depth_count - 1 + has_above.astype(jnp.int32) + has_below.astype(jnp.int32)
    pl.semaphore_wait(barrier, peers)

    def remote(source, target, send, recv, device):
        return pltpu.make_async_remote_copy(
            src_ref=source, dst_ref=target, send_sem=send, recv_sem=recv,
            device_id=device, device_id_type=pl.DeviceIdType.MESH,
        )

    def upward(p, s, c):
        return remote(to_up.at[p, s, c], from_below.at[p, s, c],
                      z_send.at[0, p, s, c], z_recv.at[0, p, s, c], (depth, lat + 1))

    def downward(p, s, c):
        return remote(to_down.at[p, s, c], from_above.at[p, s, c],
                      z_send.at[1, p, s, c], z_recv.at[1, p, s, c], (depth, lat - 1))

    def inward(p, s, c):
        place = depth * slab + s
        return remote(merged.at[p, s, c], patches.at[place, c],
                      in_send.at[p, s, c], in_recv.at[place, c], (owner(p), lat))

    def outward(s, c):
        layer = lax.rem(s, slab)
        place = jnp.minimum(slot, owned - 1)
        return remote(terms.at[s, c], home.at[place, layer, c],
                      out_send.at[s, c], out_recv.at[place, layer, c], (s // slab, lat))

    def back_up(p, s, c):
        return remote(home.at[p, s, c], terms_below.at[p, s, c],
                      back_send.at[0, p, s, c], back_recv.at[0, p, s, c], (depth, lat + 1))

    def back_down(p, s, c):
        return remote(home.at[p, s, c], terms_above.at[p, s, c],
                      back_send.at[1, p, s, c], back_recv.at[1, p, s, c], (depth, lat - 1))

    window = 2
    chunks = [(p, s, c) for s in range(slab) for p in range(owned) for c in range(2)]

    def start_pair(above, below, chunk):
        pl.when(has_above)(lambda: above(*chunk).start())
        pl.when(has_below)(lambda: below(*chunk).start())

    def sent_pair(above, below, chunk):
        pl.when(has_above)(lambda: above(*chunk).wait_send())
        pl.when(has_below)(lambda: below(*chunk).wait_send())

    for chunk in chunks[:window]:
        start_pair(upward, downward, chunk)
    for n, (p, s, c) in enumerate(chunks):
        sent_pair(upward, downward, (p, s, c))
        if n + window < len(chunks):
            start_pair(upward, downward, chunks[n + window])
        merged[p, s, c] = mine[p, s, c]

        @pl.when(has_below)
        def _():
            upward(p, s, c).wait_recv()
            merged[p, s, c] += from_below[p, s, c]

        @pl.when(has_above)
        def _():
            downward(p, s, c).wait_recv()
            merged[p, s, c] += from_above[p, s, c]

        @pl.when(owner(p) == depth)
        def _():
            patches[depth * slab + s, c] = merged[p, s, c]

        @pl.when(owner(p) != depth)
        def _():
            inward(p, s, c).start()

    @pl.when(active)
    def _():
        held[0] = probe[0]
        held[1] = probe[1]

        def exit_wave(s):
            a, b = held[0], held[1]
            psi[s, 0] = a
            psi[s, 1] = b

            @pl.when(s // slab != depth)
            def _():
                for c in range(2):
                    remote(merged.at[0, 0, c], patches.at[s, c], in_send.at[0, 0, c],
                           in_recv.at[s, c], (depth, lat)).wait_recv()

            c, d = patches[s, 0], patches[s, 1]
            return c * a - d * b, c * b + d * a

        def propagate(re, im, sign):
            re, im = transform(re, im, tables, False)
            hr, hi = wave_table[0], wave_table[1]
            if sign > 0:
                re, im = hr * re - hi * im, hr * im + hi * re
            else:
                re, im = hr * re + hi * im, hr * im - hi * re
            re, im = inverse_transform(re, im, tables)
            held[0] = re
            held[1] = im

        @pl.loop(0, count - 1)
        def _(s):
            re, im = exit_wave(s)
            propagate(re, im, 1)

        re, im = exit_wave(count - 1)
        re, im = transform(re, im, tables, False)
        target = measured[0]
        for p in range(1, owned):
            target = jnp.where(slot == p, measured[p], target)
        misfit = re * re + im * im - target
        re, im = inverse_transform(misfit * re, misfit * im, tables)
        held[0] = re
        held[1] = im

        def term(s):
            a, b = held[0], held[1]
            c, d = psi[s, 0], psi[s, 1]
            terms[s, 0] = c * a + d * b
            terms[s, 1] = c * b - d * a

            @pl.when(s // slab != depth)
            def _():
                for c in range(2):
                    outward(s, c).start()

            return a, b

        @pl.loop(0, count - 1)
        def _(i):
            s = count - 1 - i
            a, b = term(s)
            c, d = patches[s, 0], patches[s, 1]
            propagate(c * a + d * b, c * b - d * a, -1)

        term(0)

    back = [(p, s, c) for s in reversed(range(slab)) for p in range(owned) for c in range(2)]
    for n, (p, s, c) in enumerate(back):

        @pl.when(owner(p) == depth)
        def _():
            home[p, s, c] = terms[depth * slab + s, c]

        @pl.when(owner(p) != depth)
        def _():
            remote(terms.at[0, c], home.at[p, s, c], out_send.at[0, c],
                   out_recv.at[p, s, c], (depth, lat)).wait_recv()

        if n >= window:
            sent_pair(back_up, back_down, back[n - window])
        start_pair(back_up, back_down, (p, s, c))

    for chunk in back[-window:]:
        sent_pair(back_up, back_down, chunk)
    for p, s, c in back:
        pl.when(has_below)(lambda: back_up(p, s, c).wait_recv())
        pl.when(has_above)(lambda: back_down(p, s, c).wait_recv())
        pl.when(owner(p) != depth)(lambda: inward(p, s, c).wait_send())

    @pl.when(active)
    def _():
        @pl.loop(0, count)
        def _(s):
            @pl.when(s // slab != depth)
            def _():
                for c in range(2):
                    outward(s, c).wait_send()


def local(probe, prop_phase, object_field, measured, offsets):
    width = probe.shape[-1]
    slab, columns = object_field.shape[1], object_field.shape[3]
    owned = offsets.shape[0]
    depth_count = lax.axis_size("depth")
    lat_count = lax.axis_size("lat")
    depth = lax.axis_index("depth")
    lat = lax.axis_index("lat")
    tables = dft_tables(width)

    up = [(i, i + 1) for i in range(lat_count - 1)]
    down = [(i + 1, i) for i in range(lat_count - 1)]
    below = lax.ppermute(offsets, "lat", up)
    above = lax.ppermute(offsets, "lat", down)
    slot = (depth - lat * owned) % depth_count
    place = jnp.stack(
        [lat, jnp.int32(lat_count), jnp.int32(-(lat_count + 2) * width), slot]
    ).astype(jnp.int32)
    smem = pl.BlockSpec(memory_space=pltpu.SMEM)
    vmem = pl.BlockSpec(memory_space=pltpu.VMEM)
    field_spec = pl.BlockSpec((2, 1, width, columns), lambda s: (0, s, 0, 0))
    piece_spec = pl.BlockSpec((owned, 1, 2, width, width), lambda s: (0, s, 0, 0, 0))
    pieces = jax.ShapeDtypeStruct((owned, slab, 2, width, width), jnp.float32)
    limit = 56 * 1024 * 1024
    whole = pl.BlockSpec(probe.shape, lambda s: (0, 0, 0))
    mine, to_up, to_down, rolled, wave_table = pl.pallas_call(
        extract_kernel,
        grid=(slab,),
        out_shape=[pieces] * 3 + [jax.ShapeDtypeStruct(probe.shape, jnp.float32)] * 2,
        in_specs=[smem] * 4
        + [whole, pl.BlockSpec(prop_phase.shape, lambda s: (0, 0)), field_spec],
        out_specs=[piece_spec] * 3 + [whole] * 2,
        compiler_params=pltpu.CompilerParams(vmem_limit_bytes=limit),
    )(place, offsets, below, above, probe, prop_phase, object_field)

    layers = (depth_count * slab, 2, width, width)
    dma = pltpu.SemaphoreType.DMA
    home, terms_below, terms_above = pl.pallas_call(
        functools.partial(wave_kernel, depth_count, lat_count),
        out_shape=[pieces] * 3,
        in_specs=[vmem] * 7,
        out_specs=[vmem] * 3,
        scratch_shapes=[pltpu.VMEM(pieces.shape, jnp.float32)] * 3
        + [pltpu.VMEM(layers, jnp.float32)] * 3
        + [
            pltpu.VMEM(layers[1:], jnp.float32),
            dma((2, owned, slab, 2)), dma((2, owned, slab, 2)),
            dma((owned, slab, 2)), dma((layers[0], 2)),
            dma((layers[0], 2)), dma((owned, slab, 2)),
            dma((2, owned, slab, 2)), dma((2, owned, slab, 2)),
        ],
        compiler_params=pltpu.CompilerParams(
            vmem_limit_bytes=limit, collective_id=0, has_side_effects=True
        ),
    )(rolled, wave_table, tables, measured, mine, to_up, to_down)

    return pl.pallas_call(
        deposit_kernel,
        grid=(slab,),
        out_shape=jax.ShapeDtypeStruct(object_field.shape, jnp.float32),
        in_specs=[smem] * 4 + [piece_spec] * 3,
        out_specs=field_spec,
        compiler_params=pltpu.CompilerParams(vmem_limit_bytes=limit),
    )(place, offsets, below, above, home, terms_below, terms_above)


def solution(mesh):
    in_specs = (P(), P(), P(None, "depth", "lat", None), P("lat", None, None), P("lat", None))
    out_specs = P(None, "depth", "lat", None)
    return jax.shard_map(local, mesh=mesh, in_specs=in_specs, out_specs=out_specs, check_vma=False)
```
